512 devices in a mesh: head: 8 (over x, y_hi), seq: 64 (over y_lo, z, core).
Axes of the slice: x: 4, y: 4 (y_hi: 2, y_lo: 2; y = y_hi * 2 + y_lo), z: 16, core: 2. Of those that a mesh axis runs over, the one named last changes fastest.
Arguments:
- queries: bfloat16 [32768, 8192], P(('seq', 'head')), may hold values from -42.5 to 42.5
- key_states: bfloat16 [32768, 1024], P(('seq', 'head')), may hold values from -4 to 4
- value_states: bfloat16 [32768, 1024], P(('seq', 'head')), may hold values from -4 to 4
- out_grads: bfloat16 [32768, 8192], P(('seq', 'head')), may hold values from -4 to 4
- segment_ids: int32 [32768], replicated, may hold values from 0 to 7, as said below
Outputs:
- query_grads: float32 [32768, 8192], P(('seq', 'head'))
- key_grads: float32 [32768, 1024], P(('seq', 'head'))
- value_grads: float32 [32768, 1024], P(('seq', 'head'))
The draws below stay inside these ranges and needn't reach their ends.
Inputs may be any that keep to these rules, and one draw needn't show every extreme that they name: `segment_ids`: document ids never fall along positions and every one of the 8 documents has at least one position; the last document, 7, holds exactly the positions from 15872 to the end.
All inputs are finite; a program needn't handle non-finite values.
Results may differ from the reference program's by a relative error of at most 0.025.
Values may be sent and summed in bfloat16 or wider, within the bound.
No kernel may reach another device: no remote copies, remote signals or barrier semaphores. Data moves between devices by JAX's collectives and lax.ppermute only.
A program may use at most 64 MiB of HBM per device.

```python
import math
import jax
import jax.numpy as jnp
from jax import lax

HQ = 64
HK = 8
DH = 128
STRETCH = 256
DOCS = 8
PAIRS = 64
SEQ = 32768


def shared_rows(key):
    shape = (SEQ, HK, DH)
    drawn = jax.random.truncated_normal(jax.random.fold_in(key, 101), -4.0, 4.0, shape, jnp.float32)
    return drawn


def draw_key_states(key, part):
    drawn = shared_rows(key)
    result = drawn
    return result.reshape(SEQ, HK * DH).astype(jnp.bfloat16)


def draw_queries(key, part):
    key = jax.random.fold_in(key, 11)
    shape = (SEQ, HK, HQ // HK, DH)
    result = jax.random.truncated_normal(key, -4.0, 4.0, shape, jnp.float32)
    return result.reshape(SEQ, HQ * DH).astype(jnp.bfloat16)


def draw_segment_ids(key, part):
    key = jax.random.fold_in(key, 7)
    last_start = SEQ // 2 - 2 * STRETCH
    picks = jax.random.permutation(key, jnp.arange(1, last_start, dtype=jnp.int32))[:DOCS - 2]
    cuts = jnp.sort(picks)
    spots = jnp.arange(SEQ, dtype=jnp.int32)
    ids = jnp.sum((spots[:, None] >= cuts[None, :]).astype(jnp.int32), axis=1)
    ids = jnp.where(spots >= last_start, DOCS - 1, ids)
    return ids.astype(jnp.int32)


def block_scale(rng, extent, cuts, least, high):
    gain = 1.0
    for axis_at, blocks in cuts:
        draws = jax.random.uniform(jax.random.fold_in(jax.random.fold_in(rng, 6), axis_at), (blocks,), jnp.float32, least / len(cuts), high / len(cuts))
        gain = gain * jnp.repeat(jnp.exp(draws), extent[axis_at] // blocks).reshape((-1,) + (1,) * (len(extent) - 1 - axis_at))
    return gain


def centred(stream_key, dims, scale, reach, cuts=(), kind=jnp.bfloat16):
    entries = jax.random.normal(stream_key, dims, jnp.float32) * scale
    if len(cuts) > 0:
        entries = block_scale(stream_key, dims, cuts, -0.22, 0.18) * entries
    return jnp.clip(entries, min=-reach, max=reach).astype(kind)


def setup_inputs(seed: int = 0) -> dict:
    key_of = jax.random.split(jax.random.key(seed), 6)
    queries = draw_queries(jax.random.fold_in(key_of[5], 71), 0)
    key_states = draw_key_states(jax.random.fold_in(key_of[5], 71), 0)
    value_states = centred(key_of[2], (SEQ, HK * DH), 1.0, 4.0, ((0, 512),))
    out_grads = centred(key_of[3], (SEQ, HQ * DH), 1.0, 4.0, ((0, 512),))
    segment_ids = draw_segment_ids(jax.random.fold_in(key_of[5], 71), 0)
    return dict(queries=queries, key_states=key_states, value_states=value_states, out_grads=out_grads, segment_ids=segment_ids)


neg_fill = -1e+30

def pair_layout(pair_index, segment_ids):
    offsets = jnp.arange(STRETCH, dtype=jnp.int32)
    first_start = (pair_index * STRETCH).astype(jnp.int32)
    second_start = ((2 * PAIRS - 1 - pair_index) * STRETCH).astype(jnp.int32)
    positions = jnp.concatenate([first_start + offsets, second_start + offsets]).astype(jnp.int32)
    documents = jnp.concatenate([lax.dynamic_slice_in_dim(segment_ids, first_start, STRETCH, 0), lax.dynamic_slice_in_dim(segment_ids, second_start, STRETCH, 0)])
    return (positions, documents)

def one_pair(pair_index, queries, key_states, value_states, out_grads, segment_ids):
    pair_span = 2 * STRETCH
    group_size = HQ // HK
    prior_pair = ((pair_index + PAIRS - 1) % PAIRS).astype(jnp.int32)
    own_start = (pair_index * pair_span).astype(jnp.int32)
    prior_start = (prior_pair * pair_span).astype(jnp.int32)
    query_rows = lax.dynamic_slice_in_dim(queries, own_start, pair_span, 0)
    query_rows = query_rows.reshape(pair_span, HK, group_size, DH).astype(jnp.float32)
    grad_rows = lax.dynamic_slice_in_dim(out_grads, own_start, pair_span, 0)
    grad_rows = grad_rows.reshape(pair_span, HK, group_size, DH).astype(jnp.float32)
    key_rows = jnp.concatenate([lax.dynamic_slice_in_dim(key_states, own_start, pair_span, 0), lax.dynamic_slice_in_dim(key_states, prior_start, pair_span, 0)])
    key_rows = key_rows.reshape(2 * pair_span, HK, DH).astype(jnp.float32)
    value_rows = jnp.concatenate([lax.dynamic_slice_in_dim(value_states, own_start, pair_span, 0), lax.dynamic_slice_in_dim(value_states, prior_start, pair_span, 0)])
    value_rows = value_rows.reshape(2 * pair_span, HK, DH).astype(jnp.float32)
    own_positions, own_documents = pair_layout(pair_index, segment_ids)
    prior_positions, prior_documents = pair_layout(prior_pair, segment_ids)
    key_positions = jnp.concatenate([own_positions, prior_positions])
    key_documents = jnp.concatenate([own_documents, prior_documents])
    allowed = (key_positions[None, :] <= own_positions[:, None]) & (key_documents[None, :] == own_documents[:, None])
    factor = 1.0 / math.sqrt(DH)
    scores = jnp.einsum('rjgd,kjd->jgrk', query_rows, key_rows) * factor
    scores = jnp.where(allowed, scores, neg_fill)
    row_peak = lax.optimization_barrier(jnp.max(scores, axis=3, keepdims=True))
    log_total = row_peak + jnp.log(lax.optimization_barrier(jnp.sum(jnp.exp(scores - row_peak), axis=3, keepdims=True)))
    weights = jnp.where(allowed, jnp.exp(scores - log_total), 0.0)
    weights_low = lax.optimization_barrier(weights.astype(jnp.bfloat16)).astype(jnp.float32)
    output = jnp.einsum('jgrk,kjd->rjgd', weights_low, value_rows)
    row_delta = lax.optimization_barrier(jnp.sum(grad_rows * output, axis=3))
    weight_grads = jnp.einsum('rjgd,kjd->jgrk', grad_rows, value_rows)
    score_grads = weights * (weight_grads - jnp.transpose(row_delta, (1, 2, 0))[..., None])
    score_low = lax.optimization_barrier(score_grads.astype(jnp.bfloat16)).astype(jnp.float32)
    query_grad = jnp.einsum('jgrk,kjd->rjgd', score_low, key_rows) * factor
    key_grad = jnp.einsum('jgrk,rjgd->kjd', score_low, query_rows) * factor
    value_grad = jnp.einsum('jgrk,rjgd->kjd', weights_low, grad_rows)
    return (query_grad.reshape(pair_span, HQ * DH), key_grad.reshape(2 * pair_span, HK * DH), value_grad.reshape(2 * pair_span, HK * DH))

def reference(queries, key_states, value_states, out_grads, segment_ids):
    pair_span = 2 * STRETCH
    pair_ids = jnp.arange(PAIRS, dtype=jnp.int32)

    def per_pair(pair_index):
        return one_pair(pair_index, queries, key_states, value_states, out_grads, segment_ids)
    query_grad, key_grad, value_grad = lax.map(per_pair, pair_ids)
    key_total = key_grad[:, :pair_span] + jnp.roll(key_grad[:, pair_span:], -1, axis=0)
    value_total = value_grad[:, :pair_span] + jnp.roll(value_grad[:, pair_span:], -1, axis=0)
    return (query_grad.reshape(SEQ, HQ * DH), key_total.reshape(SEQ, HK * DH), value_total.reshape(SEQ, HK * DH))
```

```python
import math

import jax
import jax.numpy as jnp
from jax import lax
from jax.experimental import pallas as pl
from jax.experimental.pallas import tpu as pltpu
from jax.sharding import Mesh, PartitionSpec as P

HQ = 64
HK = 8
DH = 128
STRETCH = 256
GROUP = HQ // HK
PAIRS = 64
ROWS = 64

FACTOR = 1.0 / math.sqrt(DH)
LOG2E = 1.4426950408889634
FILL = -1e30

TEAM = ("core", "xl", "yh")
CHAIN = ("xh", "yl", "z")

OWN0, OWN1, FROM_PREV, EXTRA0, EXTRA1 = (i * STRETCH for i in range(5))


def chain_pairs():
    last = PAIRS // 2 - 1
    late = PAIRS // 2
    forward = [(n, n + 1) for n in range(last)] + [(last, late)]
    extra = [(last, late + last), (late + last, late)]
    return forward, extra


def back(pairs):
    return [(b, a) for a, b in pairs]


def nt_dot(a, b):
    return lax.dot_general(a, b, (((1,), (1,)), ((), ())), preferred_element_type=jnp.float32)


def nn_dot(a, b):
    return lax.dot_general(a, b, (((1,), (0,)), ((), ())), preferred_element_type=jnp.float32)


def attend_kernel(
    spot_ref, rows_ref, own_ref, prev_ref, extra_ref, seg_ref,
    dq_ref, down_ref, dprev_ref, dextra_ref,
    kv, kt, acc, bias,
):
    late = spot_ref[0]
    n = spot_ref[1]
    last = PAIRS // 2 - 1
    kv[0:512, :] = own_ref[...]
    kv[512:768, :] = prev_ref[...]
    kv[768:1280, :] = extra_ref[...]
    acc[...] = jnp.zeros_like(acc)
    kt[...] = kv[:, 0:DH].astype(jnp.float32).T.astype(jnp.bfloat16)

    def block_of(pair, is_late):
        return jnp.where(is_late == 1, 2 * PAIRS - 1 - pair, pair)

    def fill_bias(place, q_block, k_block):
        q_doc = jnp.broadcast_to(seg_ref[pl.ds(q_block, 1), :], (STRETCH, STRETCH))
        k_doc = jnp.broadcast_to(seg_ref[pl.ds(k_block, 1), :], (STRETCH, STRETCH))
        k_doc = k_doc.astype(jnp.float32).T
        k_pos = k_block * STRETCH + lax.broadcasted_iota(jnp.int32, (STRETCH, STRETCH), 0)
        q_pos = q_block * STRETCH + lax.broadcasted_iota(jnp.int32, (STRETCH, STRETCH), 1)
        ok = (k_pos <= q_pos) & (k_doc == q_doc.astype(jnp.float32))
        bias[place] = jnp.where(ok, 0.0, FILL)

    def run(q_base, q_block, offsets, blocks):
        count = len(offsets)
        for i in range(count):
            fill_bias(i, q_block, blocks[i])

        @pl.loop(0, GROUP)
        def _(h):
            col = pl.multiple_of(h * DH, DH)
            q = rows_ref[q_base : q_base + STRETCH, pl.ds(col, DH)]
            g = rows_ref[q_base : q_base + STRETCH, pl.ds(GROUP * DH + col, DH)]
            scores = [
                nt_dot(kv[pl.ds(o, STRETCH), 0:DH], q) * (FACTOR * LOG2E) + bias[i]
                for i, o in enumerate(offsets)
            ]
            peak = jnp.max(scores[0], axis=0, keepdims=True)
            for s in scores[1:]:
                peak = jnp.maximum(peak, jnp.max(s, axis=0, keepdims=True))
            exps = [jnp.exp2(s - peak) for s in scores]
            wgrads = [nt_dot(kv[pl.ds(o, STRETCH), DH : 2 * DH], g) for o in offsets]
            total = sum(jnp.sum(e, axis=0, keepdims=True) for e in exps)
            delta = sum(jnp.sum(e * w, axis=0, keepdims=True) for e, w in zip(exps, wgrads))
            inverse = 1.0 / total
            delta = delta * inverse
            dq_t = None
            for o, e, w in zip(offsets, exps, wgrads):
                weights = e * inverse
                score_grads = (weights * (w - delta)).astype(jnp.bfloat16)
                acc[pl.ds(o, STRETCH), 0:DH] += nn_dot(score_grads, q)
                acc[pl.ds(o, STRETCH), DH : 2 * DH] += nn_dot(weights.astype(jnp.bfloat16), g)
                part = nn_dot(kt[:, pl.ds(o, STRETCH)], score_grads)
                dq_t = part if dq_t is None else dq_t + part
            dq_ref[q_base : q_base + STRETCH, pl.ds(col, DH)] = (
                (dq_t * FACTOR).T.astype(jnp.bfloat16)
            )

    pair0 = 2 * n
    pair1 = 2 * n + 1
    b0 = block_of(pair0, late)
    b1 = block_of(pair1, late)
    head = (late == 1) & (n == 0)
    tail = (late == 1) & (n == last)
    early = late == 0
    plain_late = (late == 1) & (n != 0) & (n != last)
    end_early = PAIRS - 1
    end_late = PAIRS

    @pl.when((early & (n == 0)) | plain_late)
    def _():
        run(0, b0, [OWN0], [b0])

    @pl.when((early & (n > 0)) | tail)
    def _():
        off = pl.multiple_of(jnp.where(early, FROM_PREV, EXTRA0), STRETCH)
        run(0, b0, [OWN0, off], [b0, jnp.where(early, pair0 - 1, end_early - 1)])

    @pl.when(head)
    def _():
        run(0, b0, [OWN0, FROM_PREV, EXTRA1], [b0, end_early, end_late])

    @pl.when((late == 1) & (n != last))
    def _():
        run(STRETCH, b1, [OWN1], [b1])

    @pl.when(early)
    def _():
        run(STRETCH, b1, [OWN1, OWN0], [b1, b0])

    @pl.when(tail)
    def _():
        run(STRETCH, b1, [OWN1, EXTRA0, EXTRA1], [b1, end_early - 1, end_early])

    down_ref[:, 0:DH] = acc[0:512, 0:DH] * FACTOR
    down_ref[:, DH : 2 * DH] = acc[0:512, DH : 2 * DH]
    dprev_ref[:, 0:DH] = (acc[512:768, 0:DH] * FACTOR).astype(jnp.bfloat16)
    dprev_ref[:, DH : 2 * DH] = acc[512:768, DH : 2 * DH].astype(jnp.bfloat16)
    dextra_ref[:, 0:DH] = (acc[768:1280, 0:DH] * FACTOR).astype(jnp.bfloat16)
    dextra_ref[:, DH : 2 * DH] = acc[768:1280, DH : 2 * DH].astype(jnp.bfloat16)


def attend(spot, rows, own, prev, extra, seg):
    vmem = pl.BlockSpec(memory_space=pltpu.VMEM)
    return pl.pallas_call(
        attend_kernel,
        out_shape=(
            jax.ShapeDtypeStruct((512, GROUP * DH), jnp.bfloat16),
            jax.ShapeDtypeStruct((512, 2 * DH), jnp.float32),
            jax.ShapeDtypeStruct((256, 2 * DH), jnp.bfloat16),
            jax.ShapeDtypeStruct((512, 2 * DH), jnp.bfloat16),
        ),
        in_specs=[pl.BlockSpec(memory_space=pltpu.SMEM)] + [vmem] * 5,
        out_specs=(vmem,) * 4,
        scratch_shapes=[
            pltpu.VMEM((1280, 2 * DH), jnp.bfloat16),
            pltpu.VMEM((DH, 1280), jnp.bfloat16),
            pltpu.VMEM((1280, 2 * DH), jnp.float32),
            pltpu.VMEM((3, STRETCH, STRETCH), jnp.float32),
        ],
        compiler_params=pltpu.CompilerParams(vmem_limit_bytes=32 * 1024 * 1024),
        cost_estimate=pl.CostEstimate(
            flops=2 * 5 * 4 * 8 * 256 * 256 * 128, bytes_accessed=6 * 2**20,
            transcendentals=4 * 8 * 256 * 256,
        ),
        name="attend",
    )(spot, rows, own, prev, extra, seg)


def on_device(queries, key_states, value_states, out_grads, segment_ids):
    forward, extra = chain_pairs()

    def split_heads(array):
        return jnp.swapaxes(array.reshape(ROWS, HK, -1), 0, 1)

    with jax.named_scope("keys_out"):
        kv = jnp.concatenate([split_heads(key_states), split_heads(value_states)], axis=2)
        kv = lax.all_to_all(kv, TEAM, 0, 0, tiled=True).reshape(512, 2 * DH)
    with jax.named_scope("rows_out"):
        rows = jnp.concatenate([split_heads(queries), split_heads(out_grads)], axis=2)
        rows = lax.all_to_all(rows, TEAM, 0, 0, tiled=True).reshape(512, 2 * GROUP * DH)
    with jax.named_scope("neighbour_keys"):
        kv_prev = lax.ppermute(kv[STRETCH:], CHAIN, forward)
        kv_extra = lax.ppermute(kv, CHAIN, extra)
    spot = jnp.stack(
        [lax.axis_index("xh"), lax.axis_index("yl") * 16 + lax.axis_index("z")]
    ).astype(jnp.int32)
    seg = segment_ids.reshape(2 * PAIRS, STRETCH)
    dq, down, dprev, dextra = attend(spot, rows, kv, kv_prev, kv_extra, seg)
    with jax.named_scope("neighbour_grads"):
        from_next = lax.ppermute(dprev, CHAIN, back(forward)).astype(jnp.float32)
        from_extra = lax.ppermute(dextra, CHAIN, back(extra)).astype(jnp.float32)
        total = down + from_extra + jnp.pad(from_next, ((STRETCH, 0), (0, 0)))
        total = total.astype(jnp.bfloat16).reshape(HK, ROWS, 2 * DH)
    with jax.named_scope("grads_back"):
        sent = jnp.concatenate([dq.reshape(HK, ROWS, GROUP * DH), total], axis=2)
        got = lax.all_to_all(sent, TEAM, 0, 0, tiled=True)
        got = jnp.swapaxes(got, 0, 1).astype(jnp.float32)
        query_grads = got[:, :, : GROUP * DH].reshape(ROWS, HQ * DH)
        key_grads = got[:, :, GROUP * DH : GROUP * DH + DH].reshape(ROWS, HK * DH)
        value_grads = got[:, :, GROUP * DH + DH :].reshape(ROWS, HK * DH)
    return query_grads, key_grads, value_grads


def solution(mesh):
    cut = Mesh(
        mesh.devices.reshape(2, 2, 2, 2, 16, 2), ("xh", "xl", "yh", "yl", "z", "core")
    )
    tokens = P(("yl", "z", "core", "xh", "xl", "yh"), None)
    return jax.shard_map(
        on_device,
        mesh=cut,
        in_specs=(tokens, tokens, tokens, tokens, P()),
        out_specs=(tokens, tokens, tokens),
        check_vma=False,
    )
```

```python
import math

import jax
import jax.numpy as jnp
from jax import lax
from jax.experimental import pallas as pl
from jax.experimental.pallas import tpu as pltpu
from jax.sharding import Mesh, PartitionSpec as P

HQ = 64
HK = 8
DH = 128
STRETCH = 256
GROUP = HQ // HK
PAIRS = 64
ROWS = 64
WIDE = GROUP * DH
LAST = PAIRS // 2 - 1

FACTOR = 1.0 / math.sqrt(DH)
LOG2E = 1.4426950408889634
FILL = -1e30

TEAM = ("core", "xl", "yh")
CHAIN = ("xh", "xl", "yl", "z")

OWN0, OWN1, NEAR, FAR = (i * STRETCH for i in range(4))


def chain_pairs():
    def at(late, xl, n):
        return (late * 2 + xl) * (PAIRS // 2) + n

    odd, odd_extra, even_extra = [], [], []
    for xl in (0, 1):
        odd += [(at(0, xl, n), at(0, xl, n + 1)) for n in range(LAST)]
        odd += [(at(0, xl, LAST), at(1, 1 - xl, 0))]
        odd_extra += [(at(0, xl, LAST), at(1, 1 - xl, LAST)), (at(1, xl, LAST), at(1, xl, 0))]
        even_extra += [(at(0, xl, LAST), at(1, 1 - xl, LAST))]
    return odd, odd_extra, even_extra


def back(pairs):
    return [(b, a) for a, b in pairs]


def nt_dot(a, b):
    return lax.dot_general(a, b, (((1,), (1,)), ((), ())), preferred_element_type=jnp.float32)


def nn_dot(a, b):
    return lax.dot_general(a, b, (((1,), (0,)), ((), ())), preferred_element_type=jnp.float32)


def x_head(label, core):
    return label * 2 + core


def y_head(yh, core):
    return HK // 2 + yh * 2 + core


def span(start, size):
    return pl.ds(pl.multiple_of(start, size), size)


def labels():
    late, xl, yh, core = (lax.axis_index(name) for name in ("xh", "xl", "yh", "core"))
    n = lax.axis_index("yl") * 16 + lax.axis_index("z")
    return late, n, xl, yh, core, jnp.where(late == 1, 1 - xl, xl)


def kinds(core):
    _, _, _, yh, _, lab = labels()
    return x_head(lab, core), x_head(1 - lab, core), y_head(yh, core), y_head(1 - yh, core)


def pack_kernel(k_ref, v_ref, q_ref, g_ref, kv_ref, keep_ref, swap_ref, x_ref, y_ref):
    late = lax.axis_index("xh")
    for core in (0, 1):
        for xl in (0, 1):
            for yh in (0, 1):
                d = core * 4 + xl * 2 + yh
                hx = x_head(jnp.where(late == 1, 1 - xl, xl), core)
                hy = y_head(yh, core)
                kv_ref[d, :, 0:DH] = k_ref[:, span(hx * DH, DH)]
                kv_ref[d, :, DH : 2 * DH] = v_ref[:, span(hx * DH, DH)]
                kv_ref[d, :, 2 * DH : 3 * DH] = k_ref[:, hy * DH : hy * DH + DH]
                kv_ref[d, :, 3 * DH : 4 * DH] = v_ref[:, hy * DH : hy * DH + DH]
    core = lax.axis_index("core")
    near = (keep_ref.at[0], x_ref, keep_ref.at[1], y_ref)
    for bit, outs in ((1 - core, [swap_ref.at[i] for i in range(4)]), (core, near)):
        for out, head in zip(outs, kinds(bit)):
            out[:, 0:WIDE] = q_ref[:, span(head * WIDE, WIDE)]
            out[:, WIDE : 2 * WIDE] = g_ref[:, span(head * WIDE, WIDE)]


def attend_kernel(
    x_ref, y_ref, keep_ref, got_ref, own_ref, prev_ref, odd_ref, even_ref, seg_ref,
    dq_near, dq_swap, dq_x, dq_y, down_ref, dnear_ref, dfar_ref,
    rows, dq, kv, kt, acc, bias, arrived,
):
    late, n, xl, yh, core, _ = labels()
    early = late == 0
    first = (late == 1) & (n == 0)
    final = (late == 1) & (n == LAST)

    pieces = []
    for i, pair in ((0, core), (1, 1 - core)):
        pieces.append((x_ref.at[i], rows.at[0, pair, 1 - xl]))
        pieces.append((y_ref.at[i], rows.at[1, pair, 1 - yh]))
    copies = [pltpu.make_async_copy(a, b, arrived.at[i]) for i, (a, b) in enumerate(pieces)]
    for copy in copies:
        copy.start()
    rows[0, core, xl] = keep_ref[0]
    rows[0, 1 - core, xl] = got_ref[0]
    rows[1, core, yh] = keep_ref[1]
    rows[1, 1 - core, yh] = got_ref[2]

    def stage(at, ref, row):
        for part in (0, 1):
            block = ref[row : row + STRETCH, part * 2 * DH : (part + 1) * 2 * DH]
            kv[part, at : at + STRETCH, :] = block
            kt[part, :, at : at + STRETCH] = block[:, 0:DH].T
            acc[part, at : at + STRETCH, :] = jnp.zeros((STRETCH, 2 * DH), jnp.float32)

    stage(OWN0, own_ref, 0)
    stage(OWN1, own_ref, STRETCH)

    @pl.when(early | first)
    def _():
        stage(NEAR, prev_ref, 0)

    @pl.when(final)
    def _():
        stage(NEAR, even_ref, 0)

    @pl.when(first | final)
    def _():
        stage(FAR, odd_ref, 0)

    for copy in copies:
        copy.wait()

    def doc_row(block):
        return jnp.concatenate(
            [seg_ref[pl.ds(2 * block, 1), :], seg_ref[pl.ds(2 * block + 1, 1), :]], axis=1
        )

    def fill_bias(place, part, q_block, k_block):
        docs = doc_row(q_block)
        even = jnp.concatenate([docs[:, 0:64], docs[:, 128:192]], axis=1)
        odd = jnp.concatenate([docs[:, 64:128], docs[:, 192:256]], axis=1)
        x_doc = jnp.where(yh == 0, even, odd)
        y_doc = jnp.where(xl == 0, docs[:, :DH], docs[:, DH:])
        q_doc = jnp.where(part == 0, x_doc, y_doc).astype(jnp.float32)
        k_doc = jnp.broadcast_to(doc_row(k_block), (DH, STRETCH))
        k_doc = k_doc.astype(jnp.float32).T
        lane = lax.broadcasted_iota(jnp.int32, (STRETCH, DH), 1)
        x_row = lane + jnp.where(lane >= ROWS, ROWS, 0) + yh * ROWS
        q_pos = q_block * STRETCH + jnp.where(part == 0, x_row, lane + xl * DH)
        k_pos = k_block * STRETCH + lax.broadcasted_iota(jnp.int32, (STRETCH, DH), 0)
        ok = (k_pos <= q_pos) & (k_doc == q_doc)
        bias[place] = jnp.where(ok, 0.0, FILL)

    def unit(part, pair, offsets):
        def stack(base, h0):
            return jnp.concatenate(
                [
                    rows[part, pair, s, :, base + h * DH : base + (h + 1) * DH]
                    for h in range(h0, h0 + 2)
                    for s in (0, 1)
                ],
                axis=0,
            )

        def products(h0):
            q, g = stack(0, h0), stack(WIDE, h0)
            scores = [nt_dot(kv[part, pl.ds(o, STRETCH), 0:DH], q) for o in offsets]
            wgrads = [nt_dot(kv[part, pl.ds(o, STRETCH), DH : 2 * DH], g) for o in offsets]
            return q, g, scores, wgrads

        def softmax(scores, wgrads):
            scores = [
                s * (FACTOR * LOG2E) + jnp.concatenate([bias[i]] * 2, axis=1)
                for i, s in enumerate(scores)
            ]
            peak = jnp.max(scores[0], axis=0, keepdims=True)
            for s in scores[1:]:
                peak = jnp.maximum(peak, jnp.max(s, axis=0, keepdims=True))
            exps = [jnp.exp2(s - peak) for s in scores]
            total = sum(jnp.sum(e, axis=0, keepdims=True) for e in exps)
            delta = sum(jnp.sum(e * w, axis=0, keepdims=True) for e, w in zip(exps, wgrads))
            inverse = 1.0 / total
            delta = delta * inverse
            weights = [e * inverse for e in exps]
            grads = [(p * (w - delta)).astype(jnp.bfloat16) for p, w in zip(weights, wgrads)]
            return [p.astype(jnp.bfloat16) for p in weights], grads

        def spread(h0, q, g, weights, grads):
            dq_t = sum(nn_dot(kt[part, :, pl.ds(o, STRETCH)], d) for o, d in zip(offsets, grads))
            dq_rows = (dq_t * FACTOR).T.astype(jnp.bfloat16)
            for h in range(2):
                for s in (0, 1):
                    at = (2 * h + s) * ROWS
                    dq[part, pair, s, :, (h0 + h) * DH : (h0 + h + 1) * DH] = dq_rows[at : at + ROWS]
            return [nn_dot(d, q) for d in grads], [nn_dot(p, g) for p in weights]

        outs = []
        ahead = products(0)
        for step in range(4):
            this = ahead
            if step < 3:
                ahead = products(2 * step + 2)
            outs.append(spread(2 * step, *this[:2], *softmax(*this[2:])))

        for i, o in enumerate(offsets):
            acc[part, pl.ds(o, STRETCH), 0:DH] += sum(k[i] for k, _ in outs)
            acc[part, pl.ds(o, STRETCH), DH : 2 * DH] += sum(v[i] for _, v in outs)

    def run(pair, q_block, offsets, blocks):
        @pl.loop(0, 2)
        def _(part):
            for i in range(len(offsets)):
                fill_bias(i, part, q_block, blocks[i])
            unit(part, pair, offsets)

    def block_of(pair):
        return jnp.where(early, pair, 2 * PAIRS - 1 - pair)

    b0 = block_of(2 * n)
    b1 = block_of(2 * n + 1)
    end_early = PAIRS - 1
    end_late = PAIRS

    @pl.when((early & (n == 0)) | ((late == 1) & (n != 0) & (n != LAST)))
    def _():
        run(0, b0, [OWN0], [b0])

    @pl.when((early & (n > 0)) | final)
    def _():
        run(0, b0, [OWN0, NEAR], [b0, jnp.where(early, 2 * n - 1, end_early - 1)])

    @pl.when(first)
    def _():
        run(0, b0, [OWN0, NEAR, FAR], [b0, end_early, end_late])

    @pl.when((late == 1) & (n != LAST))
    def _():
        run(1, b1, [OWN1], [b1])

    @pl.when(early)
    def _():
        run(1, b1, [OWN1, OWN0], [b1, b0])

    @pl.when(final)
    def _():
        run(1, b1, [OWN1, NEAR, FAR], [b1, end_early - 1, end_early])

    dq_near[0] = dq[0, core, xl]
    dq_near[1] = dq[1, core, yh]
    dq_x[...] = dq[0, core, 1 - xl]
    dq_y[...] = dq[1, core, 1 - yh]
    dq_swap[0] = dq[0, 1 - core, xl]
    dq_swap[1] = dq[0, 1 - core, 1 - xl]
    dq_swap[2] = dq[1, 1 - core, yh]
    dq_swap[3] = dq[1, 1 - core, 1 - yh]

    def give(out, at, size):
        for part in (0, 1):
            k_cols = slice(part * 2 * DH, part * 2 * DH + DH)
            v_cols = slice(part * 2 * DH + DH, (part + 1) * 2 * DH)
            out[:, k_cols] = (acc[part, at : at + size, 0:DH] * FACTOR).astype(out.dtype)
            out[:, v_cols] = acc[part, at : at + size, DH : 2 * DH].astype(out.dtype)

    give(down_ref, OWN0, 512)

    @pl.when(early | first | final)
    def _():
        give(dnear_ref, NEAR, 256)

    @pl.when(first | final)
    def _():
        give(dfar_ref, FAR, 256)


def unpack_rows_kernel(dq_near, got_ref, x_ref, y_ref, q_out):
    _, _, _, yh, core, lab = labels()

    def put(head, block):
        q_out[:, span(head * WIDE, WIDE)] = block.astype(jnp.float32)

    put(x_head(lab, core), dq_near[0])
    put(x_head(lab, 1 - core), got_ref[0])
    put(y_head(yh, core), dq_near[1])
    put(y_head(yh, 1 - core), got_ref[2])
    for i, bit in ((0, core), (1, 1 - core)):
        put(x_head(1 - lab, bit), x_ref[i])
        put(y_head(1 - yh, bit), y_ref[i])


def unpack_keys_kernel(kv_ref, k_out, v_out):
    late = lax.axis_index("xh")

    def term(c, x, y, at):
        return kv_ref[c * 4 + x * 2 + y, :, at * DH : (at + 1) * DH].astype(jnp.float32)

    for c in (0, 1):
        for b in (0, 1):
            hx = x_head(jnp.where(late == 1, 1 - b, b), c)
            k_out[:, span(hx * DH, DH)] = term(c, b, 0, 0) + term(c, b, 1, 0)
            v_out[:, span(hx * DH, DH)] = term(c, b, 0, 1) + term(c, b, 1, 1)
            hy = y_head(b, c)
            k_out[:, hy * DH : hy * DH + DH] = term(c, 0, b, 2) + term(c, 1, b, 2)
            v_out[:, hy * DH : hy * DH + DH] = term(c, 0, b, 3) + term(c, 1, b, 3)


def call(kernel, name, inputs, outputs, scratch=(), limit=32, moved=1024, outside=0):
    vmem = pl.BlockSpec(memory_space=pltpu.VMEM)
    return pl.pallas_call(
        kernel,
        out_shape=tuple(jax.ShapeDtypeStruct(s, d) for s, d in outputs),
        in_specs=[pl.BlockSpec(memory_space=pl.ANY)] * outside + [vmem] * (len(inputs) - outside),
        out_specs=(vmem,) * len(outputs),
        scratch_shapes=list(scratch),
        compiler_params=pltpu.CompilerParams(vmem_limit_bytes=limit * 2**20),
        cost_estimate=pl.CostEstimate(flops=0, bytes_accessed=moved, transcendentals=0),
        name=name,
    )(*inputs)


def on_device(queries, key_states, value_states, out_grads, segment_ids):
    odd, odd_extra, even_extra = chain_pairs()
    low, wide = jnp.bfloat16, jnp.float32

    def swap(array, axis):
        return lax.ppermute(array, axis, [(0, 1), (1, 0)])

    four = ((4, ROWS, 2 * WIDE), low)
    two = ((2, ROWS, 2 * WIDE), low)
    one = ((ROWS, 2 * WIDE), low)
    kv, keep, sent, x_rows, y_rows = call(
        pack_kernel, "pack", (key_states, value_states, queries, out_grads),
        [((8, ROWS, 4 * DH), low), two, four, one, one], limit=60,
    )
    kv = lax.all_to_all(kv, TEAM, 0, 0, tiled=True).reshape(512, 4 * DH)
    got = swap(sent, "core")
    x_rows = jnp.stack([x_rows, got[1]])
    y_rows = jnp.stack([y_rows, got[3]])
    x_rows = swap(x_rows, "xl")
    y_rows = swap(y_rows, "yh")
    kv_prev = lax.ppermute(kv[STRETCH:], CHAIN, odd)
    kv_odd = lax.ppermute(kv[STRETCH:], CHAIN, odd_extra)
    kv_even = lax.ppermute(kv[:STRETCH], CHAIN, even_extra)
    seg = segment_ids.reshape(4 * PAIRS, DH)

    one = ((ROWS, WIDE), low)
    two = ((2, ROWS, WIDE), low)
    four = ((4, ROWS, WIDE), low)
    dq_near, sent, dq_x, dq_y, down, dnear, dfar = call(
        attend_kernel, "attend",
        (x_rows, y_rows, keep, got, kv, kv_prev, kv_odd, kv_even, seg),
        [two, four, one, one, ((512, 4 * DH), wide)] + [((256, 4 * DH), low)] * 2,
        scratch=[
            pltpu.VMEM((2, 2, 2, ROWS, 2 * WIDE), low),
            pltpu.VMEM((2, 2, 2, ROWS, WIDE), low),
            pltpu.VMEM((2, 4 * STRETCH, 2 * DH), low),
            pltpu.VMEM((2, DH, 4 * STRETCH), low),
            pltpu.VMEM((2, 4 * STRETCH, 2 * DH), wide),
            pltpu.VMEM((3, STRETCH, DH), wide),
            pltpu.SemaphoreType.DMA((4,)),
        ],
        limit=40, outside=2,
    )
    from_next = lax.ppermute(dnear, CHAIN, back(odd))
    from_even = lax.ppermute(dnear, CHAIN, back(even_extra))
    from_odd = lax.ppermute(dfar, CHAIN, back(odd_extra))
    got = swap(sent, "core")
    dq_x = jnp.stack([dq_x, got[1]])
    dq_y = jnp.stack([dq_y, got[3]])
    dq_x = swap(dq_x, "xl")
    dq_y = swap(dq_y, "yh")
    dq_x, dq_y, from_next, from_even, from_odd = lax.optimization_barrier(
        (dq_x, dq_y, from_next, from_even, from_odd)
    )
    add = jnp.concatenate(
        [from_even.astype(wide), from_next.astype(wide) + from_odd.astype(wide)], axis=0
    )
    total = (down + add).astype(low).reshape(HK, ROWS, 4 * DH)
    total = lax.all_to_all(total, TEAM, 0, 0, tiled=True)
    (query_grads,) = call(
        unpack_rows_kernel, "unpack_rows", (dq_near, got, dq_x, dq_y),
        [((ROWS, HQ * DH), wide)], moved=32 * 2**20,
    )
    query_grads, total = lax.optimization_barrier((query_grads, total))
    key_grads, value_grads = call(
        unpack_keys_kernel, "unpack_keys", (total,), [((ROWS, HK * DH), wide)] * 2
    )
    return query_grads, key_grads, value_grads


def solution(mesh):
    cut = Mesh(
        mesh.devices.reshape(2, 2, 2, 2, 16, 2), ("xh", "xl", "yh", "yl", "z", "core")
    )
    tokens = P(("yl", "z", "core", "xh", "xl", "yh"), None)
    return jax.shard_map(
        on_device,
        mesh=cut,
        in_specs=(tokens, tokens, tokens, tokens, P()),
        out_specs=(tokens, tokens, tokens),
        check_vma=False,
    )
```

```python
import math

import jax
import jax.numpy as jnp
from jax import lax
from jax.experimental import pallas as pl
from jax.experimental.pallas import tpu as pltpu
from jax.sharding import Mesh, PartitionSpec as P

HQ = 64
HK = 8
DH = 128
STRETCH = 256
GROUP = HQ // HK
PAIRS = 64
ROWS = 64
WIDE = GROUP * DH
LAST = PAIRS // 2 - 1

FACTOR = 1.0 / math.sqrt(DH)
LOG2E = 1.4426950408889634
FILL = -1e30

TEAM = ("core", "xl", "yh")
CHAIN = ("xh", "xl", "yl", "z")

OWN0, OWN1, NEAR, FAR = (i * STRETCH for i in range(4))


def chain_pairs():
    def at(late, xl, n):
        return (late * 2 + xl) * (PAIRS // 2) + n

    odd, odd_extra, even_extra = [], [], []
    for xl in (0, 1):
        odd += [(at(0, xl, n), at(0, xl, n + 1)) for n in range(LAST)]
        odd += [(at(0, xl, LAST), at(1, 1 - xl, 0))]
        odd_extra += [(at(0, xl, LAST), at(1, 1 - xl, LAST)), (at(1, xl, LAST), at(1, xl, 0))]
        even_extra += [(at(0, xl, LAST), at(1, 1 - xl, LAST))]
    return odd, odd_extra, even_extra


def back(pairs):
    return [(b, a) for a, b in pairs]


def nt_dot(a, b):
    return lax.dot_general(a, b, (((1,), (1,)), ((), ())), preferred_element_type=jnp.float32)


def nn_dot(a, b):
    return lax.dot_general(a, b, (((1,), (0,)), ((), ())), preferred_element_type=jnp.float32)


def x_head(label, core):
    return label * 2 + core


def y_head(yh, core):
    return HK // 2 + yh * 2 + core


def span(start, size):
    return pl.ds(pl.multiple_of(start, size), size)


def labels():
    late, xl, yh, core = (lax.axis_index(name) for name in ("xh", "xl", "yh", "core"))
    n = lax.axis_index("yl") * 16 + lax.axis_index("z")
    return late, n, xl, yh, core, jnp.where(late == 1, 1 - xl, xl)


def kinds(core):
    _, _, _, yh, _, lab = labels()
    return x_head(lab, core), x_head(1 - lab, core), y_head(yh, core), y_head(1 - yh, core)


def pack_kernel(
    q_ref, g_ref, k_ref, v_ref, kv_ref, keep_ref, swap_ref, x_ref, y_ref, arrived
):
    late, core = lax.axis_index("xh"), lax.axis_index("core")
    near = (keep_ref.at[0], x_ref, keep_ref.at[1], y_ref)
    copies = []
    for bit, outs in ((1 - core, [swap_ref.at[i] for i in range(4)]), (core, near)):
        for out, head in zip(outs, kinds(bit)):
            for ref, at in ((q_ref, 0), (g_ref, WIDE)):
                copies.append(
                    pltpu.make_async_copy(
                        ref.at[:, span(head * WIDE, WIDE)],
                        out.at[:, pl.ds(at, WIDE)],
                        arrived.at[len(copies)],
                    )
                )
    for copy in copies:
        copy.start()
    for to in (0, 1):
        for xl in (0, 1):
            for yh in (0, 1):
                d = to * 4 + xl * 2 + yh
                hx = x_head(jnp.where(late == 1, 1 - xl, xl), to)
                hy = y_head(yh, to)
                kv_ref[d, :, 0:DH] = k_ref[:, span(hx * DH, DH)]
                kv_ref[d, :, DH : 2 * DH] = v_ref[:, span(hx * DH, DH)]
                kv_ref[d, :, 2 * DH : 3 * DH] = k_ref[:, hy * DH : hy * DH + DH]
                kv_ref[d, :, 3 * DH : 4 * DH] = v_ref[:, hy * DH : hy * DH + DH]
    for copy in copies:
        copy.wait()


def attend_kernel(
    y_ref, x_ref, keep_ref, got_ref, own_ref, even_ref, odd_ref, prev_ref, seg_ref,
    dq_near, dq_swap, dq_x, dq_y, down_ref, dnear_ref, dfar_ref,
    rows, dq, kv, kt, acc, bias, arrived,
):
    late, n, xl, yh, core, _ = labels()
    early = late == 0
    first = (late == 1) & (n == 0)
    final = (late == 1) & (n == LAST)

    pieces = []
    for i, pair in ((0, core), (1, 1 - core)):
        pieces.append((x_ref.at[i], rows.at[0, pair, 1 - xl]))
        pieces.append((y_ref.at[i], rows.at[1, pair, 1 - yh]))
    copies = [pltpu.make_async_copy(a, b, arrived.at[i]) for i, (a, b) in enumerate(pieces)]
    for copy in copies:
        copy.start()
    rows[0, core, xl] = keep_ref[0]
    rows[0, 1 - core, xl] = got_ref[0]
    rows[1, core, yh] = keep_ref[1]
    rows[1, 1 - core, yh] = got_ref[2]

    def stage(at, ref, row):
        for part in (0, 1):
            block = ref[row : row + STRETCH, part * 2 * DH : (part + 1) * 2 * DH]
            kv[part, at : at + STRETCH, :] = block
            kt[part, :, at : at + STRETCH] = block[:, 0:DH].T
            acc[part, at : at + STRETCH, :] = jnp.zeros((STRETCH, 2 * DH), jnp.float32)

    stage(OWN0, own_ref, 0)
    stage(OWN1, own_ref, STRETCH)

    @pl.when(early | first)
    def _():
        stage(NEAR, prev_ref, 0)

    @pl.when(final)
    def _():
        stage(NEAR, even_ref, 0)

    @pl.when(first | final)
    def _():
        stage(FAR, odd_ref, 0)

    for copy in copies:
        copy.wait()

    def doc_row(block):
        return jnp.concatenate(
            [seg_ref[pl.ds(2 * block, 1), :], seg_ref[pl.ds(2 * block + 1, 1), :]], axis=1
        )

    def fill_bias(place, part, q_block, k_block):
        docs = doc_row(q_block)
        even = jnp.concatenate([docs[:, 0:64], docs[:, 128:192]], axis=1)
        odd = jnp.concatenate([docs[:, 64:128], docs[:, 192:256]], axis=1)
        x_doc = jnp.where(yh == 0, even, odd)
        y_doc = jnp.where(xl == 0, docs[:, :DH], docs[:, DH:])
        q_doc = jnp.where(part == 0, x_doc, y_doc).astype(jnp.float32)
        k_doc = jnp.broadcast_to(doc_row(k_block), (DH, STRETCH))
        k_doc = k_doc.astype(jnp.float32).T
        lane = lax.broadcasted_iota(jnp.int32, (STRETCH, DH), 1)
        x_row = lane + jnp.where(lane >= ROWS, ROWS, 0) + yh * ROWS
        q_pos = q_block * STRETCH + jnp.where(part == 0, x_row, lane + xl * DH)
        k_pos = k_block * STRETCH + lax.broadcasted_iota(jnp.int32, (STRETCH, DH), 0)
        ok = (k_pos <= q_pos) & (k_doc == q_doc)
        bias[place] = jnp.where(ok, 0.0, FILL)

    def unit(part, pair, offsets):
        def stack(base, h0):
            return jnp.concatenate(
                [
                    rows[part, pair, s, :, base + h * DH : base + (h + 1) * DH]
                    for h in range(h0, h0 + 2)
                    for s in (0, 1)
                ],
                axis=0,
            )

        def products(h0):
            q, g = stack(0, h0), stack(WIDE, h0)
            scores = [nt_dot(kv[part, pl.ds(o, STRETCH), 0:DH], q) for o in offsets]
            wgrads = [nt_dot(kv[part, pl.ds(o, STRETCH), DH : 2 * DH], g) for o in offsets]
            return q, g, scores, wgrads

        def softmax(scores, wgrads):
            scores = [
                s * (FACTOR * LOG2E) + jnp.concatenate([bias[i]] * 2, axis=1)
                for i, s in enumerate(scores)
            ]
            peak = jnp.max(scores[0], axis=0, keepdims=True)
            for s in scores[1:]:
                peak = jnp.maximum(peak, jnp.max(s, axis=0, keepdims=True))
            exps = [jnp.exp2(s - peak) for s in scores]
            total = sum(jnp.sum(e, axis=0, keepdims=True) for e in exps)
            delta = sum(jnp.sum(e * w, axis=0, keepdims=True) for e, w in zip(exps, wgrads))
            inverse = 1.0 / total
            delta = delta * inverse
            weights = [e * inverse for e in exps]
            grads = [(p * (w - delta)).astype(jnp.bfloat16) for p, w in zip(weights, wgrads)]
            return [p.astype(jnp.bfloat16) for p in weights], grads

        def spread(h0, q, g, weights, grads):
            dq_t = sum(nn_dot(kt[part, :, pl.ds(o, STRETCH)], d) for o, d in zip(offsets, grads))
            dq_rows = (dq_t * FACTOR).T.astype(jnp.bfloat16)
            for h in range(2):
                for s in (0, 1):
                    at = (2 * h + s) * ROWS
                    dq[part, pair, s, :, (h0 + h) * DH : (h0 + h + 1) * DH] = dq_rows[at : at + ROWS]
            return [nn_dot(d, q) for d in grads], [nn_dot(p, g) for p in weights]

        outs = []
        ahead = products(0)
        for step in range(4):
            this = ahead
            if step < 3:
                ahead = products(2 * step + 2)
            outs.append(spread(2 * step, *this[:2], *softmax(*this[2:])))

        for i, o in enumerate(offsets):
            acc[part, pl.ds(o, STRETCH), 0:DH] += sum(k[i] for k, _ in outs)
            acc[part, pl.ds(o, STRETCH), DH : 2 * DH] += sum(v[i] for _, v in outs)

    def run(pair, q_block, offsets, blocks):
        @pl.loop(0, 2)
        def _(part):
            for i in range(len(offsets)):
                fill_bias(i, part, q_block, blocks[i])
            unit(part, pair, offsets)

    def block_of(pair):
        return jnp.where(early, pair, 2 * PAIRS - 1 - pair)

    b0 = block_of(2 * n)
    b1 = block_of(2 * n + 1)
    end_early = PAIRS - 1
    end_late = PAIRS

    @pl.when((early & (n == 0)) | ((late == 1) & (n != 0) & (n != LAST)))
    def _():
        run(0, b0, [OWN0], [b0])

    @pl.when((early & (n > 0)) | final)
    def _():
        run(0, b0, [OWN0, NEAR], [b0, jnp.where(early, 2 * n - 1, end_early - 1)])

    @pl.when(first)
    def _():
        run(0, b0, [OWN0, NEAR, FAR], [b0, end_early, end_late])

    @pl.when((late == 1) & (n != LAST))
    def _():
        run(1, b1, [OWN1], [b1])

    @pl.when(early)
    def _():
        run(1, b1, [OWN1, OWN0], [b1, b0])

    @pl.when(final)
    def _():
        run(1, b1, [OWN1, NEAR, FAR], [b1, end_early - 1, end_early])

    dq_near[0] = dq[0, core, xl]
    dq_near[1] = dq[1, core, yh]
    dq_x[...] = dq[0, core, 1 - xl]
    dq_y[...] = dq[1, core, 1 - yh]
    dq_swap[0] = dq[0, 1 - core, xl]
    dq_swap[1] = dq[0, 1 - core, 1 - xl]
    dq_swap[2] = dq[1, 1 - core, yh]
    dq_swap[3] = dq[1, 1 - core, 1 - yh]

    def give(out, at, size):
        for part in (0, 1):
            k_cols = slice(part * 2 * DH, part * 2 * DH + DH)
            v_cols = slice(part * 2 * DH + DH, (part + 1) * 2 * DH)
            out[:, k_cols] = (acc[part, at : at + size, 0:DH] * FACTOR).astype(out.dtype)
            out[:, v_cols] = acc[part, at : at + size, DH : 2 * DH].astype(out.dtype)

    give(down_ref, OWN0, 512)

    @pl.when(early | first | final)
    def _():
        give(dnear_ref, NEAR, 256)

    @pl.when(first | final)
    def _():
        give(dfar_ref, FAR, 256)


def unpack_rows_kernel(dq_near, got_ref, y_ref, x_ref, q_out):
    _, _, _, yh, core, lab = labels()

    def put(head, block):
        q_out[:, span(head * WIDE, WIDE)] = block.astype(jnp.float32)

    put(x_head(lab, core), dq_near[0])
    put(x_head(lab, 1 - core), got_ref[0])
    put(y_head(yh, core), dq_near[1])
    put(y_head(yh, 1 - core), got_ref[2])
    for i, bit in ((0, core), (1, 1 - core)):
        put(x_head(1 - lab, bit), x_ref[i])
        put(y_head(1 - yh, bit), y_ref[i])


def unpack_keys_kernel(kv_ref, k_out, v_out):
    late = lax.axis_index("xh")

    def term(c, x, y, at):
        return kv_ref[c * 4 + x * 2 + y, :, at * DH : (at + 1) * DH].astype(jnp.float32)

    for c in (0, 1):
        for b in (0, 1):
            hx = x_head(jnp.where(late == 1, 1 - b, b), c)
            k_out[:, span(hx * DH, DH)] = term(c, b, 0, 0) + term(c, b, 1, 0)
            v_out[:, span(hx * DH, DH)] = term(c, b, 0, 1) + term(c, b, 1, 1)
            hy = y_head(b, c)
            k_out[:, hy * DH : hy * DH + DH] = term(c, 0, b, 2) + term(c, 1, b, 2)
            v_out[:, hy * DH : hy * DH + DH] = term(c, 0, b, 3) + term(c, 1, b, 3)


def call(kernel, name, inputs, outputs, scratch=(), limit=32, moved=1024, outside=0):
    vmem = pl.BlockSpec(memory_space=pltpu.VMEM)
    return pl.pallas_call(
        kernel,
        out_shape=tuple(jax.ShapeDtypeStruct(s, d) for s, d in outputs),
        in_specs=[pl.BlockSpec(memory_space=pl.ANY)] * outside + [vmem] * (len(inputs) - outside),
        out_specs=(vmem,) * len(outputs),
        scratch_shapes=list(scratch),
        compiler_params=pltpu.CompilerParams(vmem_limit_bytes=limit * 2**20),
        cost_estimate=pl.CostEstimate(flops=0, bytes_accessed=moved, transcendentals=0),
        name=name,
    )(*inputs)


def on_device(queries, key_states, value_states, out_grads, segment_ids):
    odd, odd_extra, even_extra = chain_pairs()
    low, wide = jnp.bfloat16, jnp.float32

    def swap(array, axis):
        return lax.ppermute(array, axis, [(0, 1), (1, 0)])

    four = ((4, ROWS, 2 * WIDE), low)
    two = ((2, ROWS, 2 * WIDE), low)
    one = ((ROWS, 2 * WIDE), low)
    kv, keep, sent, x_rows, y_rows = call(
        pack_kernel, "pack", (queries, out_grads, key_states, value_states),
        [((8, ROWS, 4 * DH), low), two, four, one, one],
        scratch=[pltpu.SemaphoreType.DMA((16,))], limit=60, outside=2,
    )
    kv = lax.all_to_all(kv, TEAM, 0, 0, tiled=True).reshape(512, 4 * DH)
    got = swap(sent, "core")
    x_rows = jnp.stack([x_rows, got[1]])
    y_rows = jnp.stack([y_rows, got[3]])
    x_rows = swap(x_rows, "xl")
    y_rows = swap(y_rows, "yh")
    kv_prev = lax.ppermute(kv[STRETCH:], CHAIN, odd)
    kv_odd = lax.ppermute(kv[STRETCH:], CHAIN, odd_extra)
    kv_even = lax.ppermute(kv[:STRETCH], CHAIN, even_extra)
    seg = segment_ids.reshape(4 * PAIRS, DH)

    one = ((ROWS, WIDE), low)
    two = ((2, ROWS, WIDE), low)
    four = ((4, ROWS, WIDE), low)
    dq_near, sent, dq_x, dq_y, down, dnear, dfar = call(
        attend_kernel, "attend",
        (y_rows, x_rows, keep, got, kv, kv_even, kv_odd, kv_prev, seg),
        [two, four, one, one, ((512, 4 * DH), wide)] + [((256, 4 * DH), low)] * 2,
        scratch=[
            pltpu.VMEM((2, 2, 2, ROWS, 2 * WIDE), low),
            pltpu.VMEM((2, 2, 2, ROWS, WIDE), low),
            pltpu.VMEM((2, 4 * STRETCH, 2 * DH), low),
            pltpu.VMEM((2, DH, 4 * STRETCH), low),
            pltpu.VMEM((2, 4 * STRETCH, 2 * DH), wide),
            pltpu.VMEM((3, STRETCH, DH), wide),
            pltpu.SemaphoreType.DMA((4,)),
        ],
        limit=40, outside=2,
    )
    from_next = lax.ppermute(dnear, CHAIN, back(odd))
    from_even = lax.ppermute(dnear, CHAIN, back(even_extra))
    from_odd = lax.ppermute(dfar, CHAIN, back(odd_extra))
    got = swap(sent, "core")
    dq_x = jnp.stack([dq_x, got[1]])
    dq_y = jnp.stack([dq_y, got[3]])
    dq_x = swap(dq_x, "xl")
    dq_y = swap(dq_y, "yh")
    dq_y, dq_x, from_even, from_odd, from_next = lax.optimization_barrier(
        (dq_y, dq_x, from_even, from_odd, from_next)
    )
    add = jnp.concatenate(
        [from_even.astype(wide), from_next.astype(wide) + from_odd.astype(wide)], axis=0
    )
    total = (down + add).astype(low).reshape(HK, ROWS, 4 * DH)
    total = lax.all_to_all(total, TEAM, 0, 0, tiled=True)
    (query_grads,) = call(
        unpack_rows_kernel, "unpack_rows", (dq_near, got, dq_y, dq_x),
        [((ROWS, HQ * DH), wide)], moved=32 * 2**20,
    )
    query_grads, total = lax.optimization_barrier((query_grads, total))
    key_grads, value_grads = call(
        unpack_keys_kernel, "unpack_keys", (total,), [((ROWS, HK * DH), wide)] * 2
    )
    return query_grads, key_grads, value_grads


def solution(mesh):
    cut = Mesh(
        mesh.devices.reshape(2, 2, 2, 2, 16, 2), ("xh", "xl", "yh", "yl", "z", "core")
    )
    tokens = P(("yl", "z", "core", "xh", "xl", "yh"), None)
    return jax.shard_map(
        on_device,
        mesh=cut,
        in_specs=(tokens, tokens, tokens, tokens, P()),
        out_specs=(tokens, tokens, tokens),
        check_vma=False,
    )
```

```python
import math

import jax
import jax.numpy as jnp
from jax import lax
from jax.experimental import pallas as pl
from jax.experimental.pallas import tpu as pltpu
from jax.sharding import Mesh, PartitionSpec as P

HQ = 64
HK = 8
DH = 128
STRETCH = 256
GROUP = HQ // HK
PAIRS = 64
ROWS = 64
WIDE = GROUP * DH
LAST = PAIRS // 2 - 1

FACTOR = 1.0 / math.sqrt(DH)
LOG2E = 1.4426950408889634
FILL = -1e30

TEAM = ("core", "xl", "yh")
CHAIN = ("xh", "xl", "yl", "z")

OWN0, OWN1, NEAR, FAR = (i * STRETCH for i in range(4))


def chain_pairs():
    def at(late, xl, n):
        return (late * 2 + xl) * (PAIRS // 2) + n

    odd, odd_extra, even_extra = [], [], []
    for xl in (0, 1):
        odd += [(at(0, xl, n), at(0, xl, n + 1)) for n in range(LAST)]
        odd += [(at(0, xl, LAST), at(1, 1 - xl, 0))]
        odd_extra += [(at(0, xl, LAST), at(1, 1 - xl, LAST)), (at(1, xl, LAST), at(1, xl, 0))]
        even_extra += [(at(0, xl, LAST), at(1, 1 - xl, LAST))]
    return odd, odd_extra, even_extra


def back(pairs):
    return [(b, a) for a, b in pairs]


def nt_dot(a, b):
    return lax.dot_general(a, b, (((1,), (1,)), ((), ())), preferred_element_type=jnp.float32)


def nn_dot(a, b):
    return lax.dot_general(a, b, (((1,), (0,)), ((), ())), preferred_element_type=jnp.float32)


def x_head(label, core):
    return label * 2 + core


def y_head(yh, core):
    return HK // 2 + yh * 2 + core


def span(start, size):
    return pl.ds(pl.multiple_of(start, size), size)


def labels():
    late, xl, yh, core = (lax.axis_index(name) for name in ("xh", "xl", "yh", "core"))
    n = lax.axis_index("yl") * 16 + lax.axis_index("z")
    return late, n, xl, yh, core, jnp.where(late == 1, 1 - xl, xl)


def kinds(core):
    _, _, _, yh, _, lab = labels()
    return x_head(lab, core), x_head(1 - lab, core), y_head(yh, core), y_head(1 - yh, core)


def pack_kernel(k_ref, v_ref, q_ref, g_ref, kv_ref, keep_ref, swap_ref, x_ref, y_ref):
    late = lax.axis_index("xh")
    for core in (0, 1):
        for xl in (0, 1):
            for yh in (0, 1):
                d = core * 4 + xl * 2 + yh
                hx = x_head(jnp.where(late == 1, 1 - xl, xl), core)
                hy = y_head(yh, core)
                kv_ref[d, :, 0:DH] = k_ref[:, span(hx * DH, DH)]
                kv_ref[d, :, DH : 2 * DH] = v_ref[:, span(hx * DH, DH)]
                kv_ref[d, :, 2 * DH : 3 * DH] = k_ref[:, hy * DH : hy * DH + DH]
                kv_ref[d, :, 3 * DH : 4 * DH] = v_ref[:, hy * DH : hy * DH + DH]
    core = lax.axis_index("core")
    near = (keep_ref.at[0], x_ref, keep_ref.at[1], y_ref)
    for bit, outs in ((1 - core, [swap_ref.at[i] for i in range(4)]), (core, near)):
        for out, head in zip(outs, kinds(bit)):
            out[:, 0:WIDE] = q_ref[:, span(head * WIDE, WIDE)]
            out[:, WIDE : 2 * WIDE] = g_ref[:, span(head * WIDE, WIDE)]


def attend_kernel(
    y_ref, x_ref, keep_ref, got_ref, own_ref, even_ref, odd_ref, prev_ref, seg_ref,
    dq_near, dq_swap, dq_x, dq_y, down_ref, dnear_ref, dfar_ref,
    rows, dq, kv, kt, acc, bias, arrived,
):
    late, n, xl, yh, core, _ = labels()
    early = late == 0
    first = (late == 1) & (n == 0)
    final = (late == 1) & (n == LAST)

    pieces = []
    for i, pair in ((0, core), (1, 1 - core)):
        pieces.append((x_ref.at[i], rows.at[0, pair, 1 - xl]))
        pieces.append((y_ref.at[i], rows.at[1, pair, 1 - yh]))
    copies = [pltpu.make_async_copy(a, b, arrived.at[i]) for i, (a, b) in enumerate(pieces)]
    for copy in copies:
        copy.start()
    rows[0, core, xl] = keep_ref[0]
    rows[0, 1 - core, xl] = got_ref[0]
    rows[1, core, yh] = keep_ref[1]
    rows[1, 1 - core, yh] = got_ref[2]

    def stage(at, ref, row):
        for part in (0, 1):
            block = ref[row : row + STRETCH, part * 2 * DH : (part + 1) * 2 * DH]
            kv[part, at : at + STRETCH, :] = block
            kt[part, :, at : at + STRETCH] = block[:, 0:DH].T
            acc[part, at : at + STRETCH, :] = jnp.zeros((STRETCH, 2 * DH), jnp.float32)

    stage(OWN0, own_ref, 0)
    stage(OWN1, own_ref, STRETCH)

    @pl.when(early | first)
    def _():
        stage(NEAR, prev_ref, 0)

    @pl.when(final)
    def _():
        stage(NEAR, even_ref, 0)

    @pl.when(first | final)
    def _():
        stage(FAR, odd_ref, 0)

    for copy in copies:
        copy.wait()

    def doc_row(block):
        return jnp.concatenate(
            [seg_ref[pl.ds(2 * block, 1), :], seg_ref[pl.ds(2 * block + 1, 1), :]], axis=1
        )

    def fill_bias(place, part, q_block, k_block):
        docs = doc_row(q_block)
        even = jnp.concatenate([docs[:, 0:64], docs[:, 128:192]], axis=1)
        odd = jnp.concatenate([docs[:, 64:128], docs[:, 192:256]], axis=1)
        x_doc = jnp.where(yh == 0, even, odd)
        y_doc = jnp.where(xl == 0, docs[:, :DH], docs[:, DH:])
        q_doc = jnp.where(part == 0, x_doc, y_doc).astype(jnp.float32)
        k_doc = jnp.broadcast_to(doc_row(k_block), (DH, STRETCH))
        k_doc = k_doc.astype(jnp.float32).T
        lane = lax.broadcasted_iota(jnp.int32, (STRETCH, DH), 1)
        x_row = lane + jnp.where(lane >= ROWS, ROWS, 0) + yh * ROWS
        q_pos = q_block * STRETCH + jnp.where(part == 0, x_row, lane + xl * DH)
        k_pos = k_block * STRETCH + lax.broadcasted_iota(jnp.int32, (STRETCH, DH), 0)
        ok = (k_pos <= q_pos) & (k_doc == q_doc)
        bias[place] = jnp.where(ok, 0.0, FILL)

    def unit(part, pair, offsets):
        def stack(base, h0):
            return jnp.concatenate(
                [
                    rows[part, pair, s, :, base + h * DH : base + (h + 1) * DH]
                    for h in range(h0, h0 + 2)
                    for s in (0, 1)
                ],
                axis=0,
            )

        def products(h0):
            q, g = stack(0, h0), stack(WIDE, h0)
            scores = [nt_dot(kv[part, pl.ds(o, STRETCH), 0:DH], q) for o in offsets]
            wgrads = [nt_dot(kv[part, pl.ds(o, STRETCH), DH : 2 * DH], g) for o in offsets]
            return q, g, scores, wgrads

        def softmax(scores, wgrads):
            scores = [
                s * (FACTOR * LOG2E) + jnp.concatenate([bias[i]] * 2, axis=1)
                for i, s in enumerate(scores)
            ]
            peak = jnp.max(scores[0], axis=0, keepdims=True)
            for s in scores[1:]:
                peak = jnp.maximum(peak, jnp.max(s, axis=0, keepdims=True))
            exps = [jnp.exp2(s - peak) for s in scores]
            total = sum(jnp.sum(e, axis=0, keepdims=True) for e in exps)
            delta = sum(jnp.sum(e * w, axis=0, keepdims=True) for e, w in zip(exps, wgrads))
            inverse = 1.0 / total
            delta = delta * inverse
            weights = [e * inverse for e in exps]
            grads = [(p * (w - delta)).astype(jnp.bfloat16) for p, w in zip(weights, wgrads)]
            return [p.astype(jnp.bfloat16) for p in weights], grads

        def spread(h0, q, g, weights, grads):
            dq_t = sum(nn_dot(kt[part, :, pl.ds(o, STRETCH)], d) for o, d in zip(offsets, grads))
            dq_rows = (dq_t * FACTOR).T.astype(jnp.bfloat16)
            for h in range(2):
                for s in (0, 1):
                    at = (2 * h + s) * ROWS
                    dq[part, pair, s, :, (h0 + h) * DH : (h0 + h + 1) * DH] = dq_rows[at : at + ROWS]
            return [nn_dot(d, q) for d in grads], [nn_dot(p, g) for p in weights]

        outs = []
        ahead = products(0)
        for step in range(4):
            this = ahead
            if step < 3:
                ahead = products(2 * step + 2)
            outs.append(spread(2 * step, *this[:2], *softmax(*this[2:])))

        for i, o in enumerate(offsets):
            acc[part, pl.ds(o, STRETCH), 0:DH] += sum(k[i] for k, _ in outs)
            acc[part, pl.ds(o, STRETCH), DH : 2 * DH] += sum(v[i] for _, v in outs)

    def run(pair, q_block, offsets, blocks):
        @pl.loop(0, 2)
        def _(part):
            for i in range(len(offsets)):
                fill_bias(i, part, q_block, blocks[i])
            unit(part, pair, offsets)

    def block_of(pair):
        return jnp.where(early, pair, 2 * PAIRS - 1 - pair)

    b0 = block_of(2 * n)
    b1 = block_of(2 * n + 1)
    end_early = PAIRS - 1
    end_late = PAIRS

    @pl.when((early & (n == 0)) | ((late == 1) & (n != 0) & (n != LAST)))
    def _():
        run(0, b0, [OWN0], [b0])

    @pl.when((early & (n > 0)) | final)
    def _():
        run(0, b0, [OWN0, NEAR], [b0, jnp.where(early, 2 * n - 1, end_early - 1)])

    @pl.when(first)
    def _():
        run(0, b0, [OWN0, NEAR, FAR], [b0, end_early, end_late])

    @pl.when((late == 1) & (n != LAST))
    def _():
        run(1, b1, [OWN1], [b1])

    @pl.when(early)
    def _():
        run(1, b1, [OWN1, OWN0], [b1, b0])

    @pl.when(final)
    def _():
        run(1, b1, [OWN1, NEAR, FAR], [b1, end_early - 1, end_early])

    dq_near[0] = dq[0, core, xl]
    dq_near[1] = dq[1, core, yh]
    dq_x[...] = dq[0, core, 1 - xl]
    dq_y[...] = dq[1, core, 1 - yh]
    dq_swap[0] = dq[0, 1 - core, xl]
    dq_swap[1] = dq[0, 1 - core, 1 - xl]
    dq_swap[2] = dq[1, 1 - core, yh]
    dq_swap[3] = dq[1, 1 - core, 1 - yh]

    def give(out, at, size):
        for part in (0, 1):
            k_cols = slice(part * 2 * DH, part * 2 * DH + DH)
            v_cols = slice(part * 2 * DH + DH, (part + 1) * 2 * DH)
            out[:, k_cols] = (acc[part, at : at + size, 0:DH] * FACTOR).astype(out.dtype)
            out[:, v_cols] = acc[part, at : at + size, DH : 2 * DH].astype(out.dtype)

    give(down_ref, OWN0, 512)

    @pl.when(early | first | final)
    def _():
        give(dnear_ref, NEAR, 256)

    @pl.when(first | final)
    def _():
        give(dfar_ref, FAR, 256)


def unpack_rows_kernel(dq_near, got_ref, y_ref, x_ref, q_out):
    _, _, _, yh, core, lab = labels()

    def put(head, block):
        q_out[:, span(head * WIDE, WIDE)] = block.astype(jnp.float32)

    put(x_head(lab, core), dq_near[0])
    put(x_head(lab, 1 - core), got_ref[0])
    put(y_head(yh, core), dq_near[1])
    put(y_head(yh, 1 - core), got_ref[2])
    for i, bit in ((0, core), (1, 1 - core)):
        put(x_head(1 - lab, bit), x_ref[i])
        put(y_head(1 - yh, bit), y_ref[i])


def unpack_keys_kernel(kv_ref, k_out, v_out):
    late = lax.axis_index("xh")

    def term(c, x, y, at):
        return kv_ref[c * 4 + x * 2 + y, :, at * DH : (at + 1) * DH].astype(jnp.float32)

    for c in (0, 1):
        for b in (0, 1):
            hx = x_head(jnp.where(late == 1, 1 - b, b), c)
            k_out[:, span(hx * DH, DH)] = term(c, b, 0, 0) + term(c, b, 1, 0)
            v_out[:, span(hx * DH, DH)] = term(c, b, 0, 1) + term(c, b, 1, 1)
            hy = y_head(b, c)
            k_out[:, hy * DH : hy * DH + DH] = term(c, 0, b, 2) + term(c, 1, b, 2)
            v_out[:, hy * DH : hy * DH + DH] = term(c, 0, b, 3) + term(c, 1, b, 3)


def call(kernel, name, inputs, outputs, scratch=(), limit=32, moved=1024, outside=0):
    vmem = pl.BlockSpec(memory_space=pltpu.VMEM)
    return pl.pallas_call(
        kernel,
        out_shape=tuple(jax.ShapeDtypeStruct(s, d) for s, d in outputs),
        in_specs=[pl.BlockSpec(memory_space=pl.ANY)] * outside + [vmem] * (len(inputs) - outside),
        out_specs=(vmem,) * len(outputs),
        scratch_shapes=list(scratch),
        compiler_params=pltpu.CompilerParams(vmem_limit_bytes=limit * 2**20),
        cost_estimate=pl.CostEstimate(flops=0, bytes_accessed=moved, transcendentals=0),
        name=name,
    )(*inputs)


def on_device(queries, key_states, value_states, out_grads, segment_ids):
    odd, odd_extra, even_extra = chain_pairs()
    low, wide = jnp.bfloat16, jnp.float32

    def swap(array, axis):
        return lax.ppermute(array, axis, [(0, 1), (1, 0)])

    four = ((4, ROWS, 2 * WIDE), low)
    two = ((2, ROWS, 2 * WIDE), low)
    one = ((ROWS, 2 * WIDE), low)
    kv, keep, sent, x_rows, y_rows = call(
        pack_kernel, "pack", (key_states, value_states, queries, out_grads),
        [((8, ROWS, 4 * DH), low), two, four, one, one], limit=60,
    )
    kv = lax.all_to_all(kv, TEAM, 0, 0, tiled=True).reshape(512, 4 * DH)
    got = swap(sent, "core")
    x_rows = jnp.stack([x_rows, got[1]])
    y_rows = jnp.stack([y_rows, got[3]])
    x_rows = swap(x_rows, "xl")
    y_rows = swap(y_rows, "yh")
    kv_prev = lax.ppermute(kv[STRETCH:], CHAIN, odd)
    kv_odd = lax.ppermute(kv[STRETCH:], CHAIN, odd_extra)
    kv_even = lax.ppermute(kv[:STRETCH], CHAIN, even_extra)
    seg = segment_ids.reshape(4 * PAIRS, DH)

    one = ((ROWS, WIDE), low)
    two = ((2, ROWS, WIDE), low)
    four = ((4, ROWS, WIDE), low)
    dq_near, sent, dq_x, dq_y, down, dnear, dfar = call(
        attend_kernel, "attend",
        (y_rows, x_rows, keep, got, kv, kv_even, kv_odd, kv_prev, seg),
        [two, four, one, one, ((512, 4 * DH), wide)] + [((256, 4 * DH), low)] * 2,
        scratch=[
            pltpu.VMEM((2, 2, 2, ROWS, 2 * WIDE), low),
            pltpu.VMEM((2, 2, 2, ROWS, WIDE), low),
            pltpu.VMEM((2, 4 * STRETCH, 2 * DH), low),
            pltpu.VMEM((2, DH, 4 * STRETCH), low),
            pltpu.VMEM((2, 4 * STRETCH, 2 * DH), wide),
            pltpu.VMEM((3, STRETCH, DH), wide),
            pltpu.SemaphoreType.DMA((4,)),
        ],
        limit=40, outside=2,
    )
    from_next = lax.ppermute(dnear, CHAIN, back(odd))
    from_even = lax.ppermute(dnear, CHAIN, back(even_extra))
    from_odd = lax.ppermute(dfar, CHAIN, back(odd_extra))
    got = swap(sent, "core")
    dq_x = jnp.stack([dq_x, got[1]])
    dq_y = jnp.stack([dq_y, got[3]])
    dq_x = swap(dq_x, "xl")
    dq_y = swap(dq_y, "yh")
    dq_y, dq_x, from_even, from_odd, from_next = lax.optimization_barrier(
        (dq_y, dq_x, from_even, from_odd, from_next)
    )
    add = jnp.concatenate(
        [from_even.astype(wide), from_next.astype(wide) + from_odd.astype(wide)], axis=0
    )
    total = (down + add).astype(low).reshape(HK, ROWS, 4 * DH)
    total = lax.all_to_all(total, TEAM, 0, 0, tiled=True)
    (query_grads,) = call(
        unpack_rows_kernel, "unpack_rows", (dq_near, got, dq_y, dq_x),
        [((ROWS, HQ * DH), wide)], moved=32 * 2**20,
    )
    query_grads, total = lax.optimization_barrier((query_grads, total))
    key_grads, value_grads = call(
        unpack_keys_kernel, "unpack_keys", (total,), [((ROWS, HK * DH), wide)] * 2
    )
    return query_grads, key_grads, value_grads


def solution(mesh):
    cut = Mesh(
        mesh.devices.reshape(2, 2, 2, 2, 16, 2), ("xh", "xl", "yh", "yl", "z", "core")
    )
    tokens = P(("yl", "z", "core", "xh", "xl", "yh"), None)
    return jax.shard_map(
        on_device,
        mesh=cut,
        in_specs=(tokens, tokens, tokens, tokens, P()),
        out_specs=(tokens, tokens, tokens),
        check_vma=False,
    )
```
